32 devices in a mesh: section: 8 (over z, x), neuron: 4 (over y, core).
Axes of the slice: x: 2, y: 2, z: 4, core: 2. Of those that a mesh axis runs over, the one named last changes fastest.
Arguments:
- inputs: bfloat16 [6, 32768], P(None, 'neuron'), may hold values from 0 to 2
- weight_tiles: bfloat16 [8, 2048, 128, 128], P('section', 'neuron'), may hold values from -0.07324219 to 0.07910156
- source_block: int32 [8, 2048], P('section', 'neuron'), may hold values from 0 to 255
- target_block: int32 [8, 2048], P('section', 'neuron'), may hold values from 0 to 63
- live_slots: int32 [8, 4], P('section', 'neuron'), may hold values from 64 to 512, as said below
Outputs:
- activations: bfloat16 [8, 6, 32768], P('section', None, 'neuron')
The draws below stay inside these ranges and needn't reach their ends.
Inputs may be any that keep to these rules, and one draw needn't show every extreme that they name: live_slots[l, n] is 512, 256, 128 or 64, and in every layer some shard has all 512 slots live.
All inputs are finite; a program needn't handle non-finite values.
Results may differ from the reference program's by a relative error of at most 0.0045.
Values may be sent and summed in bfloat16 or wider, within the bound.
A program may use at most 64 MiB of HBM per device.

```python
import jax
import jax.numpy as jnp
from jax import lax

NEURONS = 32768
BLOCK = 128
LAYERS = 8
NBLK = 256
COLS_DEV = 64
SLOTS = 512
SLOT_ALL = 2048
ROWS = 6
N_NEURON = 4


def draw_live_slots(key, part):
    shift_key, pick_key = jax.random.split(key)
    shifts = jax.random.randint(shift_key, (LAYERS, N_NEURON), 0, 4)
    chosen = jax.random.randint(pick_key, (LAYERS, 1), 0, N_NEURON)
    shifts = jnp.where(jnp.arange(N_NEURON)[None, :] == chosen, 0, shifts)
    return jnp.right_shift(jnp.full((LAYERS, N_NEURON), SLOTS, jnp.int32), shifts.astype(jnp.int32)).astype(jnp.int32)


def plant(values, stream_key, low, high):
    shape = values.shape
    spot = [jax.random.randint(jax.random.fold_in(stream_key, axis), (), 0, shape[axis]) for axis in range(len(shape))]
    values = values.at[tuple(spot)].set(low)
    longest = shape.index(max(shape))
    spot[longest] = (spot[longest] + 1) % shape[longest]
    return values.at[tuple(spot)].set(high)


def levels(rng, extent, cuts, smallest, top_value):
    def one(axis_at, blocks):
        heights = jax.random.uniform(jax.random.fold_in(jax.random.fold_in(rng, 6), axis_at), (blocks,), jnp.float32, smallest / len(cuts), top_value / len(cuts))
        return jnp.repeat(jnp.exp(heights), extent[axis_at] // blocks).reshape((-1,) + (1,) * (len(extent) - axis_at - 1))

    factor_of = one(*cuts[0])
    for cut in cuts[1:]:
        factor_of = factor_of * one(*cut)
    return factor_of


def setup_inputs(seed: int = 0) -> dict:
    streams_of = jax.random.split(jax.random.key(seed), 6)
    return {
        "inputs": jnp.clip(2.0 * jax.random.uniform(streams_of[0], (ROWS, NEURONS), jnp.float32) ** levels(streams_of[0], (ROWS, NEURONS), ((1, 4),), -0.2, 0.2), 0.0, 2.0).astype(jnp.bfloat16),
        "weight_tiles": jnp.clip(-0.07324219 + 0.15234375 * jax.random.uniform(streams_of[1], (LAYERS, SLOT_ALL, BLOCK, BLOCK), jnp.float32) ** levels(streams_of[1], (LAYERS, SLOT_ALL, BLOCK, BLOCK), ((0, 8), (1, 4)), -0.2, 0.2), -0.07324219, 0.07910156).astype(jnp.bfloat16),
        "source_block": plant(jax.random.randint(streams_of[2], (LAYERS, SLOT_ALL), 0, NBLK), jax.random.fold_in(streams_of[2], 1), 0, NBLK - 1).astype(jnp.int32),
        "target_block": plant(jax.random.randint(streams_of[3], (LAYERS, SLOT_ALL), 0, COLS_DEV), jax.random.fold_in(streams_of[3], 1), 0, COLS_DEV - 1).astype(jnp.int32),
        "live_slots": draw_live_slots(jax.random.fold_in(streams_of[5], 71), 0),
    }


NEURON_BIAS = -0.3
CLIP_LEVEL = 32.0


def reference(inputs, weight_tiles, source_block, target_block, live_slots):
    block_count = NEURONS // BLOCK
    row_count = inputs.shape[0]
    slot_index = jnp.arange(SLOT_ALL, dtype=jnp.int32)
    shard_of = (slot_index // SLOTS).astype(jnp.int32)
    layer_list = []
    current = inputs
    for layer_num in range(LAYERS):
        shaped = current.reshape(row_count, block_count, BLOCK).astype(jnp.float32)
        picked = jnp.take(shaped, source_block[layer_num], axis=1)
        live_mask = (slot_index - shard_of * SLOTS) < live_slots[layer_num][shard_of]
        partial_value = jnp.einsum("rsk,skj->rsj", picked, weight_tiles[layer_num].astype(jnp.float32), precision=lax.Precision.HIGHEST)
        partial_value = partial_value * live_mask.astype(jnp.float32)[None, :, None]
        target = (shard_of * COLS_DEV + target_block[layer_num]).astype(jnp.int32)
        summed = jnp.zeros((row_count, block_count, BLOCK), jnp.float32).at[:, target, :].add(partial_value)
        current = jnp.clip(summed + NEURON_BIAS, 0.0, CLIP_LEVEL).astype(jnp.bfloat16).reshape(row_count, NEURONS)
        layer_list.append(current)
    return jnp.stack(layer_list)
```

```python
import functools

import jax
import jax.numpy as jnp
from jax import lax
from jax.experimental import pallas as pl
from jax.experimental.pallas import tpu as pltpu
from jax.sharding import PartitionSpec as P

NEURON_BIAS = -0.3
CLIP_LEVEL = 32.0
CHUNKS = 3
WCHUNKS = 8
PAD = 8
MESH = pl.DeviceIdType.MESH


def kernel(sections, shards, src_ref, live_ref, tgt_ref, in_ref, w_ref, out_ref,
           wbuf, ybuf, xbuf, pbuf, wsem, sx, rx, sy, ry, ss, rs):
    rows, cols, block = in_ref.shape
    slots = wbuf.shape[0]
    chips = shards // 2
    per = rows // CHUNKS
    wper = slots // WCHUNKS
    pstride = slots + PAD
    s = lax.axis_index("section")
    n = lax.axis_index("neuron")
    y = lax.div(n, 2)
    core = lax.rem(n, 2)
    sibling = n + 1 - 2 * core

    def peer(d):
        return lax.rem(y + d, chips) * 2 + core

    def origin(d):
        return lax.rem(y + chips - d, chips) * 2

    loads = [
        pltpu.make_async_copy(
            w_ref.at[0, pl.ds(k * wper, wper)], wbuf.at[pl.ds(k * wper, wper)], wsem.at[k]
        )
        for k in range(WCHUNKS)
    ]
    for load in loads:
        load.start()

    barrier = pltpu.get_barrier_semaphore()
    pl.semaphore_signal(barrier, inc=1, device_id=(s, sibling), device_id_type=MESH)
    for d in range(1, chips):
        pl.semaphore_signal(barrier, inc=1, device_id=(s, peer(d)), device_id_type=MESH)

    @pl.when(s > 0)
    def _():
        pl.semaphore_signal(barrier, inc=1, device_id=(s - 1, n), device_id_type=MESH)

    @pl.when(s < sections - 1)
    def _():
        pl.semaphore_signal(barrier, inc=1, device_id=(s + 1, n), device_id_type=MESH)

    pl.semaphore_wait(
        barrier,
        chips + (s > 0).astype(jnp.int32) + (s < sections - 1).astype(jnp.int32),
    )

    def at_chunk(shard, k):
        return ybuf.at[shard, pl.ds(k * per, per)]

    def along(k):
        return pltpu.make_async_remote_copy(
            src_ref=out_ref.at[pl.ds(k * per, per)], dst_ref=at_chunk(n, k),
            send_sem=sx.at[k], recv_sem=rx.at[k],
            device_id=(s + 1, n), device_id_type=MESH)

    def across(d, k):
        return pltpu.make_async_remote_copy(
            src_ref=at_chunk(n, k), dst_ref=at_chunk(n, k),
            send_sem=sy.at[d - 1, k], recv_sem=ry.at[d - 1, k],
            device_id=(s, peer(d)), device_id_type=MESH)

    def beside(d, k):
        shard = origin(d) + core
        return pltpu.make_async_remote_copy(
            src_ref=at_chunk(shard, k), dst_ref=at_chunk(shard, k),
            send_sem=ss.at[d, k], recv_sem=rs.at[d, k],
            device_id=(s, sibling), device_id_type=MESH)

    def spread(shard, k):
        for i in range(per):
            r = k * per + i
            value = ybuf[shard, r].astype(jnp.float32)
            xbuf[pl.ds(shard * cols, cols), r, :] = value

    xbuf[...] = jnp.zeros_like(xbuf)
    column = lax.broadcasted_iota(jnp.int32, (cols, slots), 0)
    place = lax.broadcasted_iota(jnp.int32, (cols, slots), 1)
    chosen = (tgt_ref[...] == column) & (place < live_ref[0, 0])
    selector = chosen.astype(jnp.float32).astype(jnp.bfloat16)

    @pl.when(s == 0)
    def _():
        ybuf[n] = in_ref[...]

    for k in range(CHUNKS):
        @pl.when(s > 0)
        def _():
            along(k).wait_recv()

        for d in range(1, chips):
            across(d, k).start()
        beside(0, k).start()
        spread(n, k)
    for k in range(CHUNKS):
        for d in range(1, chips):
            across(d, k).wait_recv()
            beside(d, k).start()
            spread(origin(d) + core, k)
    for k in range(CHUNKS):
        for d in range(chips):
            beside(d, k).wait_recv()
            spread(origin(d) + 1 - core, k)

    blank = jnp.zeros((8, block), jnp.float32)

    def multiply(t):
        j = t * 4
        x = [xbuf[src_ref[0, j + i]] for i in range(4)]
        left = jnp.concatenate([
            jnp.concatenate([x[0], blank], axis=1),
            jnp.concatenate([blank, x[1]], axis=1),
            jnp.concatenate([x[2], blank], axis=1),
            jnp.concatenate([blank, x[3]], axis=1),
        ], axis=0).astype(jnp.bfloat16)
        w = [wbuf[j + i] for i in range(4)]
        right = jnp.concatenate([
            jnp.concatenate([w[0], w[2]], axis=1),
            jnp.concatenate([w[1], w[3]], axis=1),
        ], axis=0)
        product = jnp.dot(left, right, preferred_element_type=jnp.float32)
        for i in range(4):
            half = (i // 2) * block
            pbuf[pl.ds(j + i, 8, stride=pstride), :] = product[i * 8:i * 8 + 8, half:half + block]

    for k in range(WCHUNKS):
        loads[k].wait()

        @pl.loop(0, wper // 4, unroll=4)
        def _(t):
            multiply(k * (wper // 4) + t)

    for k in range(CHUNKS):
        for i in range(per):
            r = k * per + i
            part = pbuf[r * pstride:r * pstride + slots, :]
            high = part.astype(jnp.bfloat16)
            low = (part - high.astype(jnp.float32)).astype(jnp.bfloat16)
            both = jnp.dot(
                selector, jnp.concatenate([high, low], axis=1),
                preferred_element_type=jnp.float32)
            total = both[:, :block] + both[:, block:]
            out_ref[r] = jnp.clip(total + NEURON_BIAS, 0.0, CLIP_LEVEL).astype(jnp.bfloat16)

        @pl.when(s < sections - 1)
        def _():
            along(k).start()

    for k in range(CHUNKS):
        for d in range(1, chips):
            across(d, k).wait_send()
        for d in range(chips):
            beside(d, k).wait_send()

        @pl.when(s < sections - 1)
        def _():
            along(k).wait_send()


def local(sections, shards, inputs, weight_tiles, source_block, target_block, live_slots):
    rows, width = inputs.shape
    slots, block = weight_tiles.shape[1], weight_tiles.shape[2]
    cols = width // block
    chips = shards // 2
    result = pl.pallas_call(
        functools.partial(kernel, sections, shards),
        out_shape=jax.ShapeDtypeStruct((rows, cols, block), jnp.bfloat16),
        in_specs=[
            pl.BlockSpec(memory_space=pltpu.SMEM),
            pl.BlockSpec(memory_space=pltpu.SMEM),
            pl.BlockSpec(memory_space=pltpu.VMEM),
            pl.BlockSpec(memory_space=pltpu.VMEM),
            pl.BlockSpec(memory_space=pl.ANY),
        ],
        out_specs=pl.BlockSpec(memory_space=pltpu.VMEM),
        scratch_shapes=[
            pltpu.VMEM((slots, block, block), jnp.bfloat16),
            pltpu.VMEM((shards, rows, cols, block), jnp.bfloat16),
            pltpu.VMEM((shards * cols, 8, block), jnp.float32),
            pltpu.VMEM((8 * (slots + PAD), block), jnp.float32),
            pltpu.SemaphoreType.DMA((WCHUNKS,)),
            pltpu.SemaphoreType.DMA((CHUNKS,)),
            pltpu.SemaphoreType.DMA((CHUNKS,)),
            pltpu.SemaphoreType.DMA((max(chips - 1, 1), CHUNKS)),
            pltpu.SemaphoreType.DMA((max(chips - 1, 1), CHUNKS)),
            pltpu.SemaphoreType.DMA((chips, CHUNKS)),
            pltpu.SemaphoreType.DMA((chips, CHUNKS)),
        ],
        compiler_params=pltpu.CompilerParams(
            collective_id=0, has_side_effects=True, vmem_limit_bytes=48 * 1024 * 1024),
    )(source_block, live_slots, target_block, inputs.reshape(rows, cols, block), weight_tiles)
    return result.reshape(1, rows, width)


def solution(mesh):
    in_specs = (
        P(None, "neuron"),
        P("section", "neuron", None, None),
        P("section", "neuron"),
        P("section", "neuron"),
        P("section", "neuron"),
    )
    out_specs = P("section", None, "neuron")
    body = functools.partial(local, mesh.shape["section"], mesh.shape["neuron"])
    return jax.shard_map(body, mesh=mesh, in_specs=in_specs, out_specs=out_specs, check_vma=False)
```

```python
import functools

import jax
import jax.numpy as jnp
from jax import lax
from jax.experimental import pallas as pl
from jax.experimental.pallas import tpu as pltpu
from jax.sharding import PartitionSpec as P

NEURON_BIAS = -0.3
CLIP_LEVEL = 32.0
CHUNKS = 3
WCHUNKS = 4
UNROLL = 64
PAD = 8
MESH = pl.DeviceIdType.MESH


def kernel(sections, shards, src_ref, live_ref, tgt_ref, in_ref, w_ref, out_ref,
           wbuf, ybuf, xbuf, pbuf, wsem, sx, rx, sy, ss, rs):
    rows, cols, block = in_ref.shape
    slots = wbuf.shape[0]
    chips = shards // 2
    per = rows // CHUNKS
    wper = slots // WCHUNKS
    pstride = slots + PAD
    s = lax.axis_index("section")
    n = lax.axis_index("neuron")
    y = lax.div(n, 2)
    core = lax.rem(n, 2)
    sibling = n + 1 - 2 * core

    def peer(d):
        return lax.rem(y + d, chips) * 2 + core

    def origin(d):
        return lax.rem(y + chips - d, chips) * 2

    loads = [
        pltpu.make_async_copy(
            w_ref.at[0, pl.ds(k * wper, wper)], wbuf.at[pl.ds(k * wper, wper)], wsem.at[k]
        )
        for k in range(WCHUNKS)
    ]
    for load in loads:
        load.start()

    barrier = pltpu.get_barrier_semaphore()
    pl.semaphore_signal(barrier, inc=1, device_id=(s, sibling), device_id_type=MESH)

    @pl.when(s == 0)
    def _():
        for d in range(1, chips):
            pl.semaphore_signal(barrier, inc=1, device_id=(s, peer(d)), device_id_type=MESH)

    @pl.when(s > 0)
    def _():
        for d in range(chips):
            pl.semaphore_signal(barrier, inc=1, device_id=(s - 1, peer(d)), device_id_type=MESH)

    @pl.when(s < sections - 1)
    def _():
        for d in range(chips):
            pl.semaphore_signal(barrier, inc=1, device_id=(s + 1, peer(d)), device_id_type=MESH)

    first = (s == 0).astype(jnp.int32)
    last = (s == sections - 1).astype(jnp.int32)
    pl.semaphore_wait(barrier, 1 + 2 * chips - first - last * chips)

    def at_chunk(shard, k):
        return ybuf.at[shard, pl.ds(k * per, per)]

    def along(d, k):
        return pltpu.make_async_remote_copy(
            src_ref=out_ref.at[pl.ds(k * per, per)], dst_ref=at_chunk(n, k),
            send_sem=sx.at[d, k], recv_sem=rx.at[d, k],
            device_id=(s + 1, peer(d)), device_id_type=MESH)

    def across(d, k):
        return pltpu.make_async_remote_copy(
            src_ref=in_ref.at[pl.ds(k * per, per)], dst_ref=at_chunk(n, k),
            send_sem=sy.at[d, k], recv_sem=rx.at[d, k],
            device_id=(s, peer(d)), device_id_type=MESH)

    def beside(d, k):
        shard = origin(d) + core
        return pltpu.make_async_remote_copy(
            src_ref=at_chunk(shard, k), dst_ref=at_chunk(shard, k),
            send_sem=ss.at[d, k], recv_sem=rs.at[d, k],
            device_id=(s, sibling), device_id_type=MESH)

    def spread(shard, k):
        for i in range(per):
            r = k * per + i
            value = ybuf[shard, r].astype(jnp.float32)
            xbuf[pl.ds(shard * cols, cols), r, :] = value

    xbuf[...] = jnp.zeros_like(xbuf)
    column = lax.broadcasted_iota(jnp.int32, (cols, slots), 0)
    place = lax.broadcasted_iota(jnp.int32, (cols, slots), 1)
    chosen = (tgt_ref[...] == column) & (place < live_ref[0, 0])
    selector = chosen.astype(jnp.float32).astype(jnp.bfloat16)

    @pl.when(s == 0)
    def _():
        for k in range(CHUNKS):
            for d in range(1, chips):
                across(d, k).start()
        ybuf[n] = in_ref[...]

    for k in range(CHUNKS):
        @pl.when(s > 0)
        def _():
            along(0, k).wait_recv()

        beside(0, k).start()
        for d in range(1, chips):
            along(d, k).wait_recv()
            beside(d, k).start()
        for d in range(chips):
            spread(origin(d) + core, k)
    for k in range(CHUNKS):
        for d in range(chips):
            beside(d, k).wait_recv()
            spread(origin(d) + 1 - core, k)

    blank = jnp.zeros((8, block), jnp.float32)

    def multiply(t):
        j = t * 4
        x = [xbuf[src_ref[0, j + i]] for i in range(4)]
        left = jnp.concatenate([
            jnp.concatenate([x[0], blank], axis=1),
            jnp.concatenate([blank, x[1]], axis=1),
            jnp.concatenate([x[2], blank], axis=1),
            jnp.concatenate([blank, x[3]], axis=1),
        ], axis=0).astype(jnp.bfloat16)
        w = [wbuf[j + i] for i in range(4)]
        right = jnp.concatenate([
            jnp.concatenate([w[0], w[2]], axis=1),
            jnp.concatenate([w[1], w[3]], axis=1),
        ], axis=0)
        product = jnp.dot(left, right, preferred_element_type=jnp.float32)
        for i in range(4):
            half = (i // 2) * block
            pbuf[pl.ds(j + i, 8, stride=pstride), :] = product[i * 8:i * 8 + 8, half:half + block]

    for load in loads:
        load.wait()

    @pl.loop(0, slots // 4, unroll=min(UNROLL, slots // 4))
    def _(t):
        multiply(t)

    for k in range(CHUNKS):
        for i in range(per):
            r = k * per + i
            part = pbuf[r * pstride:r * pstride + slots, :]
            high = part.astype(jnp.bfloat16)
            low = (part - high.astype(jnp.float32)).astype(jnp.bfloat16)
            both = jnp.dot(
                selector, jnp.concatenate([high, low], axis=1),
                preferred_element_type=jnp.float32)
            total = both[:, :block] + both[:, block:]
            out_ref[r] = jnp.clip(total + NEURON_BIAS, 0.0, CLIP_LEVEL).astype(jnp.bfloat16)

        @pl.when(s < sections - 1)
        def _():
            for d in range(chips):
                along(d, k).start()

    @pl.when(s == 0)
    def _():
        for k in range(CHUNKS):
            for d in range(1, chips):
                across(d, k).wait_send()

    for k in range(CHUNKS):
        for d in range(chips):
            beside(d, k).wait_send()

        @pl.when(s < sections - 1)
        def _():
            for d in range(chips):
                along(d, k).wait_send()


def local(sections, shards, inputs, weight_tiles, source_block, target_block, live_slots):
    rows, width = inputs.shape
    slots, block = weight_tiles.shape[1], weight_tiles.shape[2]
    cols = width // block
    chips = shards // 2
    result = pl.pallas_call(
        functools.partial(kernel, sections, shards),
        out_shape=jax.ShapeDtypeStruct((rows, cols, block), jnp.bfloat16),
        in_specs=[
            pl.BlockSpec(memory_space=pltpu.SMEM),
            pl.BlockSpec(memory_space=pltpu.SMEM),
            pl.BlockSpec(memory_space=pltpu.VMEM),
            pl.BlockSpec(memory_space=pltpu.VMEM),
            pl.BlockSpec(memory_space=pl.ANY),
        ],
        out_specs=pl.BlockSpec(memory_space=pltpu.VMEM),
        scratch_shapes=[
            pltpu.VMEM((slots, block, block), jnp.bfloat16),
            pltpu.VMEM((shards, rows, cols, block), jnp.bfloat16),
            pltpu.VMEM((shards * cols, 8, block), jnp.float32),
            pltpu.VMEM((8 * (slots + PAD), block), jnp.float32),
            pltpu.SemaphoreType.DMA((WCHUNKS,)),
            pltpu.SemaphoreType.DMA((chips, CHUNKS)),
            pltpu.SemaphoreType.DMA((chips, CHUNKS)),
            pltpu.SemaphoreType.DMA((chips, CHUNKS)),
            pltpu.SemaphoreType.DMA((chips, CHUNKS)),
            pltpu.SemaphoreType.DMA((chips, CHUNKS)),
        ],
        compiler_params=pltpu.CompilerParams(
            collective_id=0, has_side_effects=True, vmem_limit_bytes=48 * 1024 * 1024),
    )(source_block, live_slots, target_block, inputs.reshape(rows, cols, block), weight_tiles)
    return result.reshape(1, rows, width)


def solution(mesh):
    in_specs = (
        P(None, "neuron"),
        P("section", "neuron", None, None),
        P("section", "neuron"),
        P("section", "neuron"),
        P("section", "neuron"),
    )
    out_specs = P("section", None, "neuron")
    body = functools.partial(local, mesh.shape["section"], mesh.shape["neuron"])
    return jax.shard_map(body, mesh=mesh, in_specs=in_specs, out_specs=out_specs, check_vma=False)
```

```python
import functools

import jax
import jax.numpy as jnp
from jax import lax
from jax.experimental import pallas as pl
from jax.experimental.pallas import tpu as pltpu
from jax.sharding import PartitionSpec as P

NEURON_BIAS = -0.3
CLIP_LEVEL = 32.0
CHUNKS = 6
GROUPS = 2
WCHUNKS = 4
UNROLL = 64
PAD = 8
MESH = pl.DeviceIdType.MESH


def kernel(sections, shards, src_ref, live_ref, tgt_ref, in_ref, w_ref, out_ref,
           wbuf, ybuf, xbuf, pbuf, wsem, sx, rx, sy, ss, rs):
    rows, cols, block = in_ref.shape
    slots = wbuf.shape[0]
    chips = shards // 2
    per = rows // CHUNKS
    band = rows // GROUPS
    held = CHUNKS // GROUPS
    wper = slots // WCHUNKS
    pstride = slots + PAD
    s = lax.axis_index("section")
    n = lax.axis_index("neuron")
    y = lax.div(n, 2)
    core = lax.rem(n, 2)
    sibling = n + 1 - 2 * core

    def peer(d):
        return lax.rem(y + d, chips) * 2 + core

    def origin(d):
        return lax.rem(y + chips - d, chips) * 2

    loads = [
        pltpu.make_async_copy(
            w_ref.at[0, pl.ds(k * wper, wper)], wbuf.at[pl.ds(k * wper, wper)], wsem.at[k]
        )
        for k in range(WCHUNKS)
    ]
    for load in loads:
        load.start()

    barrier = pltpu.get_barrier_semaphore()
    pl.semaphore_signal(barrier, inc=1, device_id=(s, sibling), device_id_type=MESH)

    @pl.when(s == 0)
    def _():
        for d in range(1, chips):
            pl.semaphore_signal(barrier, inc=1, device_id=(s, peer(d)), device_id_type=MESH)

    @pl.when(s > 0)
    def _():
        for d in range(chips):
            pl.semaphore_signal(barrier, inc=1, device_id=(s - 1, peer(d)), device_id_type=MESH)

    @pl.when(s < sections - 1)
    def _():
        for d in range(chips):
            pl.semaphore_signal(barrier, inc=1, device_id=(s + 1, peer(d)), device_id_type=MESH)

    first = (s == 0).astype(jnp.int32)
    last = (s == sections - 1).astype(jnp.int32)
    pl.semaphore_wait(barrier, 1 + 2 * chips - first - last * chips)

    def at_chunk(shard, k):
        return ybuf.at[shard, pl.ds(k * per, per)]

    def along(d, k):
        return pltpu.make_async_remote_copy(
            src_ref=out_ref.at[pl.ds(k * per, per)], dst_ref=at_chunk(n, k),
            send_sem=sx.at[d, k], recv_sem=rx.at[d, k],
            device_id=(s + 1, peer(d)), device_id_type=MESH)

    def across(d, k):
        return pltpu.make_async_remote_copy(
            src_ref=in_ref.at[pl.ds(k * per, per)], dst_ref=at_chunk(n, k),
            send_sem=sy.at[d, k], recv_sem=rx.at[d, k],
            device_id=(s, peer(d)), device_id_type=MESH)

    def beside(d, k):
        shard = origin(d) + core
        return pltpu.make_async_remote_copy(
            src_ref=at_chunk(shard, k), dst_ref=at_chunk(shard, k),
            send_sem=ss.at[d, k], recv_sem=rs.at[d, k],
            device_id=(s, sibling), device_id_type=MESH)

    def spread(shard, k):
        for i in range(per):
            r = k * per + i
            value = ybuf[shard, r].astype(jnp.float32)
            xbuf[pl.ds(shard * cols, cols), r % band, :] = value

    xbuf[...] = jnp.zeros_like(xbuf)
    column = lax.broadcasted_iota(jnp.int32, (cols, slots), 0)
    place = lax.broadcasted_iota(jnp.int32, (cols, slots), 1)
    chosen = (tgt_ref[...] == column) & (place < live_ref[0, 0])
    selector = chosen.astype(jnp.float32).astype(jnp.bfloat16)

    @pl.when(s == 0)
    def _():
        for k in range(CHUNKS):
            for d in range(1, chips):
                across(d, k).start()
        ybuf[n] = in_ref[...]

    def receive(g):
        for k in range(g * held, (g + 1) * held):
            @pl.when(s > 0)
            def _():
                along(0, k).wait_recv()

            beside(0, k).start()
            for d in range(1, chips):
                along(d, k).wait_recv()
                beside(d, k).start()

    def settle(g):
        for k in range(g * held, (g + 1) * held):
            for d in range(chips):
                spread(origin(d) + core, k)
        for k in range(g * held, (g + 1) * held):
            for d in range(chips):
                beside(d, k).wait_recv()
                spread(origin(d) + 1 - core, k)

    blank = jnp.zeros((8, block), jnp.float32)

    def multiply(t):
        j = t * 4
        x = [xbuf[src_ref[0, j + i]] for i in range(4)]
        left = jnp.concatenate([
            jnp.concatenate([x[0], blank], axis=1),
            jnp.concatenate([blank, x[1]], axis=1),
            jnp.concatenate([x[2], blank], axis=1),
            jnp.concatenate([blank, x[3]], axis=1),
        ], axis=0).astype(jnp.bfloat16)
        w = [wbuf[j + i] for i in range(4)]
        right = jnp.concatenate([
            jnp.concatenate([w[0], w[2]], axis=1),
            jnp.concatenate([w[1], w[3]], axis=1),
        ], axis=0)
        product = jnp.dot(left, right, preferred_element_type=jnp.float32)
        for i in range(4):
            half = (i // 2) * block
            pbuf[pl.ds(j + i, band, stride=pstride), :] = product[i * 8:i * 8 + band, half:half + block]

    def products():
        @pl.loop(0, slots // 4, unroll=min(UNROLL, slots // 4))
        def _(t):
            multiply(t)

    def finish(g):
        for k in range(g * held, (g + 1) * held):
            for r in range(k * per, (k + 1) * per):
                at = (r % band) * pstride
                part = pbuf[at:at + slots, :]
                high = part.astype(jnp.bfloat16)
                low = (part - high.astype(jnp.float32)).astype(jnp.bfloat16)
                both = jnp.dot(
                    selector, jnp.concatenate([high, low], axis=1),
                    preferred_element_type=jnp.float32)
                total = both[:, :block] + both[:, block:]
                out_ref[r] = jnp.clip(total + NEURON_BIAS, 0.0, CLIP_LEVEL).astype(jnp.bfloat16)

            @pl.when(s < sections - 1)
            def _():
                for d in range(chips):
                    along(d, k).start()

    receive(0)
    settle(0)
    for load in loads:
        load.wait()
    for g in range(GROUPS):
        products()
        if g + 1 < GROUPS:
            receive(g + 1)
        finish(g)
        if g + 1 < GROUPS:
            settle(g + 1)

    @pl.when(s == 0)
    def _():
        for k in range(CHUNKS):
            for d in range(1, chips):
                across(d, k).wait_send()

    for k in range(CHUNKS):
        for d in range(chips):
            beside(d, k).wait_send()

        @pl.when(s < sections - 1)
        def _():
            for d in range(chips):
                along(d, k).wait_send()


def local(sections, shards, inputs, weight_tiles, source_block, target_block, live_slots):
    rows, width = inputs.shape
    slots, block = weight_tiles.shape[1], weight_tiles.shape[2]
    cols = width // block
    chips = shards // 2
    result = pl.pallas_call(
        functools.partial(kernel, sections, shards),
        out_shape=jax.ShapeDtypeStruct((rows, cols, block), jnp.bfloat16),
        in_specs=[
            pl.BlockSpec(memory_space=pltpu.SMEM),
            pl.BlockSpec(memory_space=pltpu.SMEM),
            pl.BlockSpec(memory_space=pltpu.VMEM),
            pl.BlockSpec(memory_space=pltpu.VMEM),
            pl.BlockSpec(memory_space=pl.ANY),
        ],
        out_specs=pl.BlockSpec(memory_space=pltpu.VMEM),
        scratch_shapes=[
            pltpu.VMEM((slots, block, block), jnp.bfloat16),
            pltpu.VMEM((shards, rows, cols, block), jnp.bfloat16),
            pltpu.VMEM((shards * cols, 8, block), jnp.float32),
            pltpu.VMEM((8 * (slots + PAD), block), jnp.float32),
            pltpu.SemaphoreType.DMA((WCHUNKS,)),
            pltpu.SemaphoreType.DMA((chips, CHUNKS)),
            pltpu.SemaphoreType.DMA((chips, CHUNKS)),
            pltpu.SemaphoreType.DMA((chips, CHUNKS)),
            pltpu.SemaphoreType.DMA((chips, CHUNKS)),
            pltpu.SemaphoreType.DMA((chips, CHUNKS)),
        ],
        compiler_params=pltpu.CompilerParams(
            collective_id=0, has_side_effects=True, vmem_limit_bytes=48 * 1024 * 1024),
    )(source_block, live_slots, target_block, inputs.reshape(rows, cols, block), weight_tiles)
    return result.reshape(1, rows, width)


def solution(mesh):
    in_specs = (
        P(None, "neuron"),
        P("section", "neuron", None, None),
        P("section", "neuron"),
        P("section", "neuron"),
        P("section", "neuron"),
    )
    out_specs = P("section", None, "neuron")
    body = functools.partial(local, mesh.shape["section"], mesh.shape["neuron"])
    return jax.shard_map(body, mesh=mesh, in_specs=in_specs, out_specs=out_specs, check_vma=False)
```

```python
import functools

import jax
import jax.numpy as jnp
from jax import lax
from jax.experimental import pallas as pl
from jax.experimental.pallas import tpu as pltpu
from jax.sharding import PartitionSpec as P

NEURON_BIAS = -0.3
CLIP_LEVEL = 32.0
CHUNKS = 6
GROUPS = 3
WCHUNKS = 4
UNROLL = 64
PAD = 8
MESH = pl.DeviceIdType.MESH


def kernel(sections, shards, src_ref, live_ref, tgt_ref, in_ref, w_ref, out_ref,
           wbuf, ybuf, xbuf, pbuf, wsem, sx, rx, sy, ss, rs):
    rows, cols, block = in_ref.shape
    slots = wbuf.shape[0]
    chips = shards // 2
    per = rows // CHUNKS
    band = rows // GROUPS
    held = CHUNKS // GROUPS
    wper = slots // WCHUNKS
    pstride = slots + PAD
    s = lax.axis_index("section")
    n = lax.axis_index("neuron")
    y = lax.div(n, 2)
    core = lax.rem(n, 2)
    sibling = n + 1 - 2 * core

    def peer(d):
        return lax.rem(y + d, chips) * 2 + core

    def origin(d):
        return lax.rem(y + chips - d, chips) * 2

    loads = [
        pltpu.make_async_copy(
            w_ref.at[0, pl.ds(k * wper, wper)], wbuf.at[pl.ds(k * wper, wper)], wsem.at[k]
        )
        for k in range(WCHUNKS)
    ]
    for load in loads:
        load.start()

    barrier = pltpu.get_barrier_semaphore()
    pl.semaphore_signal(barrier, inc=1, device_id=(s, sibling), device_id_type=MESH)

    @pl.when(s == 0)
    def _():
        for d in range(1, chips):
            pl.semaphore_signal(barrier, inc=1, device_id=(s, peer(d)), device_id_type=MESH)

    @pl.when(s > 0)
    def _():
        for d in range(chips):
            pl.semaphore_signal(barrier, inc=1, device_id=(s - 1, peer(d)), device_id_type=MESH)

    @pl.when(s < sections - 1)
    def _():
        for d in range(chips):
            pl.semaphore_signal(barrier, inc=1, device_id=(s + 1, peer(d)), device_id_type=MESH)

    first = (s == 0).astype(jnp.int32)
    last = (s == sections - 1).astype(jnp.int32)
    pl.semaphore_wait(barrier, 1 + 2 * chips - first - last * chips)

    def at_chunk(shard, k):
        return ybuf.at[shard, pl.ds(k * per, per)]

    def along(d, k):
        return pltpu.make_async_remote_copy(
            src_ref=out_ref.at[pl.ds(k * per, per)], dst_ref=at_chunk(n, k),
            send_sem=sx.at[d, k], recv_sem=rx.at[d, k],
            device_id=(s + 1, peer(d)), device_id_type=MESH)

    def across(d, k):
        return pltpu.make_async_remote_copy(
            src_ref=in_ref.at[pl.ds(k * per, per)], dst_ref=at_chunk(n, k),
            send_sem=sy.at[d, k], recv_sem=rx.at[d, k],
            device_id=(s, peer(d)), device_id_type=MESH)

    def beside(d, k):
        shard = origin(d) + core
        return pltpu.make_async_remote_copy(
            src_ref=at_chunk(shard, k), dst_ref=at_chunk(shard, k),
            send_sem=ss.at[d, k], recv_sem=rs.at[d, k],
            device_id=(s, sibling), device_id_type=MESH)

    def spread(shard, k):
        for i in range(per):
            r = k * per + i
            value = ybuf[shard, r].astype(jnp.float32)
            xbuf[pl.ds(shard * cols, cols), r % band, :] = value

    xbuf[...] = jnp.zeros_like(xbuf)
    column = lax.broadcasted_iota(jnp.int32, (cols, slots), 0)
    place = lax.broadcasted_iota(jnp.int32, (cols, slots), 1)
    chosen = (tgt_ref[...] == column) & (place < live_ref[0, 0])
    selector = chosen.astype(jnp.float32).astype(jnp.bfloat16)

    @pl.when(s == 0)
    def _():
        for k in range(CHUNKS):
            for d in range(1, chips):
                across(d, k).start()
        ybuf[n] = in_ref[...]

    def receive(g):
        for k in range(g * held, (g + 1) * held):
            @pl.when(s > 0)
            def _():
                along(0, k).wait_recv()

            beside(0, k).start()
            for d in range(1, chips):
                along(d, k).wait_recv()
                beside(d, k).start()

    def settle(g):
        for k in range(g * held, (g + 1) * held):
            for d in range(chips):
                spread(origin(d) + core, k)
        for k in range(g * held, (g + 1) * held):
            for d in range(chips):
                beside(d, k).wait_recv()
                spread(origin(d) + 1 - core, k)

    blank = jnp.zeros((8, block), jnp.float32)

    def multiply(t):
        j = t * 4
        x = [xbuf[src_ref[0, j + i]] for i in range(4)]
        left = jnp.concatenate([
            jnp.concatenate([x[0], blank], axis=1),
            jnp.concatenate([blank, x[1]], axis=1),
            jnp.concatenate([x[2], blank], axis=1),
            jnp.concatenate([blank, x[3]], axis=1),
        ], axis=0).astype(jnp.bfloat16)
        w = [wbuf[j + i] for i in range(4)]
        right = jnp.concatenate([
            jnp.concatenate([w[0], w[2]], axis=1),
            jnp.concatenate([w[1], w[3]], axis=1),
        ], axis=0)
        product = jnp.dot(left, right, preferred_element_type=jnp.float32)
        for i in range(4):
            half = (i // 2) * block
            pbuf[pl.ds(j + i, band, stride=pstride), :] = product[i * 8:i * 8 + band, half:half + block]

    def products():
        @pl.loop(0, slots // 4, unroll=min(UNROLL, slots // 4))
        def _(t):
            multiply(t)

    def finish(g):
        for k in range(g * held, (g + 1) * held):
            for r in range(k * per, (k + 1) * per):
                at = (r % band) * pstride
                part = pbuf[at:at + slots, :]
                high = part.astype(jnp.bfloat16)
                low = (part - high.astype(jnp.float32)).astype(jnp.bfloat16)
                both = jnp.dot(
                    selector, jnp.concatenate([high, low], axis=1),
                    preferred_element_type=jnp.float32)
                total = both[:, :block] + both[:, block:]
                out_ref[r] = jnp.clip(total + NEURON_BIAS, 0.0, CLIP_LEVEL).astype(jnp.bfloat16)

            @pl.when(s < sections - 1)
            def _():
                for d in range(1, chips):
                    along(d, k).start()
                along(0, k).start()

    receive(0)
    settle(0)
    for load in loads:
        load.wait()
    for g in range(GROUPS):
        products()
        if g + 1 < GROUPS:
            receive(g + 1)
        finish(g)
        if g + 1 < GROUPS:
            settle(g + 1)

    @pl.when(s == 0)
    def _():
        for k in range(CHUNKS):
            for d in range(1, chips):
                across(d, k).wait_send()

    for k in range(CHUNKS):
        for d in range(chips):
            beside(d, k).wait_send()

        @pl.when(s < sections - 1)
        def _():
            for d in range(chips):
                along(d, k).wait_send()


def local(sections, shards, inputs, weight_tiles, source_block, target_block, live_slots):
    rows, width = inputs.shape
    slots, block = weight_tiles.shape[1], weight_tiles.shape[2]
    cols = width // block
    chips = shards // 2
    result = pl.pallas_call(
        functools.partial(kernel, sections, shards),
        out_shape=jax.ShapeDtypeStruct((rows, cols, block), jnp.bfloat16),
        in_specs=[
            pl.BlockSpec(memory_space=pltpu.SMEM),
            pl.BlockSpec(memory_space=pltpu.SMEM),
            pl.BlockSpec(memory_space=pltpu.VMEM),
            pl.BlockSpec(memory_space=pltpu.VMEM),
            pl.BlockSpec(memory_space=pl.ANY),
        ],
        out_specs=pl.BlockSpec(memory_space=pltpu.VMEM),
        scratch_shapes=[
            pltpu.VMEM((slots, block, block), jnp.bfloat16),
            pltpu.VMEM((shards, rows, cols, block), jnp.bfloat16),
            pltpu.VMEM((shards * cols, 8, block), jnp.float32),
            pltpu.VMEM((8 * (slots + PAD), block), jnp.float32),
            pltpu.SemaphoreType.DMA((WCHUNKS,)),
            pltpu.SemaphoreType.DMA((chips, CHUNKS)),
            pltpu.SemaphoreType.DMA((chips, CHUNKS)),
            pltpu.SemaphoreType.DMA((chips, CHUNKS)),
            pltpu.SemaphoreType.DMA((chips, CHUNKS)),
            pltpu.SemaphoreType.DMA((chips, CHUNKS)),
        ],
        compiler_params=pltpu.CompilerParams(
            collective_id=0, has_side_effects=True, vmem_limit_bytes=48 * 1024 * 1024),
    )(source_block, live_slots, target_block, inputs.reshape(rows, cols, block), weight_tiles)
    return result.reshape(1, rows, width)


def solution(mesh):
    in_specs = (
        P(None, "neuron"),
        P("section", "neuron", None, None),
        P("section", "neuron"),
        P("section", "neuron"),
        P("section", "neuron"),
    )
    out_specs = P("section", None, "neuron")
    body = functools.partial(local, mesh.shape["section"], mesh.shape["neuron"])
    return jax.shard_map(body, mesh=mesh, in_specs=in_specs, out_specs=out_specs, check_vma=False)
```
